512 devices in a mesh: grp: 8 (over x, y_hi), gz: 64 (over z, y_lo, core).
Axes of the slice: x: 4, y: 8 (y_hi: 2, y_lo: 4; y = y_hi * 4 + y_lo), z: 8, core: 2. Of those that a mesh axis runs over, the one named last changes fastest.
Arguments:
- init_fields: float32 [8, 12, 256, 64, 128], P('grp', None, 'gz'), may hold values from -6 to 6
- conductivity: float32 [4, 256, 64, 128], P(None, 'gz'), may hold values from 0.1 to 1
- seeds: int32 [8, 12], P('grp'), may hold values from 0 to 3
- counts: int32 [8], replicated, may hold values from 1 to 12, as said below
Outputs:
- ens_mean: float32 [256, 64, 128], P('gz', 'grp')
- ens_var: float32 [256, 64, 128], P('gz', 'grp')
- ens_third: float32 [256, 64, 128], P('gz', 'grp')
- ens_fourth: float32 [256, 64, 128], P('gz', 'grp')
The draws below stay inside these ranges and needn't reach their ends.
Inputs may be any that keep to these rules, and one draw needn't show every extreme that they name: counts[g] is how many leading slots of group g are live members; some group has all 12 slots live.
All inputs are finite; a program needn't handle non-finite values.
Results may differ from the reference program's by a relative error of at most 0.0003.
Values sent between devices are 32-bit elements; how exact they have to be, the bound alone decides.
A program may use at most 128 MiB of HBM per device.

```python
import math
import jax
import jax.numpy as jnp
from jax import lax

NX = 64
NY = 128
MEMB = 12
NFIELD = 4
STEPS = 4
GRP = 8
NZ = 256


def draw_counts(key, part):
    key = jax.random.fold_in(key, 11)
    first = jax.random.fold_in(key, 1)
    second = jax.random.fold_in(key, 2)
    base = jax.random.randint(first, (GRP,), 1, MEMB + 1)
    full = jax.random.randint(second, (), 0, GRP)
    return jnp.where(jnp.arange(GRP) == full, MEMB, base).astype(jnp.int32)


def touch_ends(array, key, smallest, top_value):
    extent = array.shape
    index_at = [jax.random.randint(jax.random.fold_in(key, axis), (), 0, extent[axis]) for axis in range(len(extent))]
    array = array.at[tuple(index_at)].set(smallest)
    longest = extent.index(max(extent))
    index_at[longest] = (index_at[longest] + 1) % extent[longest]
    return array.at[tuple(index_at)].set(top_value)


def block_levels(stream_key, dims, split, smallest, largest):
    loudness, own = 1.0, jax.random.fold_in(stream_key, 6)
    for dim, parts in split:
        steps = jnp.exp(jax.random.uniform(jax.random.fold_in(own, dim), (parts,), jnp.float32, smallest / len(split), largest / len(split)))
        loudness = loudness * jnp.repeat(steps, dims[dim] // parts).reshape([-1 if axis == dim else 1 for axis in range(len(dims))])
    return loudness


def bell_draw(stream_key, extent, scale, limit, cuts=(), held_as=jnp.bfloat16):
    factor_of = block_levels(stream_key, extent, cuts, -0.22, 0.18) if cuts else 1.0
    array = jax.random.normal(stream_key, extent, jnp.float32) * scale * factor_of
    return jnp.minimum(jnp.maximum(array, -limit), limit).astype(held_as)


def setup_inputs(seed: int = 0) -> dict:
    keys = jax.random.split(jax.random.key(seed), 5)
    return {
        "init_fields": bell_draw(keys[0], (GRP, MEMB, NZ, NX, NY), 1.0, 6.0, ((0, 8), (2, 64)), jnp.float32),
        "conductivity": jnp.clip(jnp.exp(math.log(1.0) - 2.3025851 * jax.random.uniform(keys[1], (NFIELD, NZ, NX, NY), jnp.float32) ** block_levels(keys[1], (NFIELD, NZ, NX, NY), ((1, 64),), -0.2, 0.2)), 0.1, 1.0),
        "seeds": touch_ends(jax.random.randint(keys[2], (GRP, MEMB), 0, NFIELD), jax.random.fold_in(keys[2], 1), 0, NFIELD - 1).astype(jnp.int32),
        "counts": draw_counts(jax.random.fold_in(keys[4], 71), 0),
    }


step_size = 0.15


def update(u_ext, k_ext):
    u = u_ext[:, 1:-1]
    k = k_ext[:, 1:-1]
    flux = 0.5 * (k + k_ext[:, 2:]) * (u_ext[:, 2:] - u)
    flux = flux + 0.5 * (k + k_ext[:, :-2]) * (u_ext[:, :-2] - u)
    u_pad = jnp.pad(u, ((0, 0), (0, 0), (1, 1), (1, 1)))
    k_pad = jnp.pad(k, ((0, 0), (0, 0), (1, 1), (1, 1)))
    flux = flux + 0.5 * (k + k_pad[:, :, 2:, 1:-1]) * (u_pad[:, :, 2:, 1:-1] - u)
    flux = flux + 0.5 * (k + k_pad[:, :, :-2, 1:-1]) * (u_pad[:, :, :-2, 1:-1] - u)
    flux = flux + 0.5 * (k + k_pad[:, :, 1:-1, 2:]) * (u_pad[:, :, 1:-1, 2:] - u)
    flux = flux + 0.5 * (k + k_pad[:, :, 1:-1, :-2]) * (u_pad[:, :, 1:-1, :-2] - u)
    return u + step_size * flux


def pad_z(field):
    return jnp.pad(field, ((0, 0), (1, 1), (0, 0), (0, 0)))


def member_stats(state, count):
    slots = state.shape[0]
    live = (jnp.arange(slots, dtype=jnp.int32) < count).astype(jnp.float32)[:, None, None, None]
    total = count.astype(jnp.float32)
    mean = jnp.sum(live * state, axis=0) / total
    centred = (state - mean) * live
    square = centred * centred
    return (total, mean, jnp.sum(square, axis=0), jnp.sum(square * centred, axis=0), jnp.sum(square * square, axis=0))


def chan(left, right):
    na, ma, a2, a3, a4 = left
    nb, mb, b2, b3, b4 = right
    total = na + nb
    delta = mb - ma
    ratio = delta / total
    mean = ma + ratio * nb
    cross = delta * ratio * na * nb
    m2 = a2 + b2 + cross
    m3 = a3 + b3 + cross * ratio * (na - nb) + 3.0 * ratio * (na * b2 - nb * a2)
    m4 = (a4 + b4 + cross * ratio * ratio * (na * na - na * nb + nb * nb)
          + 6.0 * ratio * ratio * (na * na * b2 + nb * nb * a2) + 4.0 * ratio * (na * b3 - nb * a3))
    return (total, mean, m2, m3, m4)


def reference(init_fields, conductivity, seeds, counts):
    def one_group(index):
        state = init_fields[index]
        coeff = jnp.take(conductivity, seeds[index], axis=0)
        coeff_ext = pad_z(coeff)
        for step in range(STEPS):
            state = update(pad_z(state), coeff_ext)
        return member_stats(state, counts[index])

    stats = lax.map(one_group, jnp.arange(GRP, dtype=jnp.int32))
    merged = tuple(s[0] for s in stats)
    for index in range(1, GRP):
        merged = chan(merged, tuple(s[index] for s in stats))
    total, mean, m2, m3, m4 = merged
    return (mean, m2 / total, m3 / total, m4 / total)
```

```python
import functools

import jax
import jax.numpy as jnp
from jax import lax
from jax.experimental import pallas as pl
from jax.experimental.pallas import tpu as pltpu
from jax.sharding import PartitionSpec as P

STEPS = 4
PAIR = 2
CHUNK = 2
HALF_STEP = 0.15 * 0.5
MESH = pl.DeviceIdType.MESH


def kernel(groups, ring, seeds_ref, counts_ref, init_ref, cond_ref,
           out_ref,
           state_0, state_1, state_2, state_3, state_4, lo_in, hi_in,
           cond, cond_lo, cond_hi, cz, cx, cy, keep,
           sums, got_x, part, got_y,
           load_sem, cond_sem, rim_send, rim_recv, x_send, x_recv, y_send, y_recv):
    members, layers, nx, ny = init_ref.shape
    fields = cond_ref.shape[0]
    columns = groups // PAIR
    share = nx // groups
    chunks = members // CHUNK
    last = layers - 1
    state = (state_0, state_1, state_2, state_3, state_4)
    g = lax.axis_index("grp")
    z = lax.axis_index("gz")
    column, half = g // PAIR, g % PAIR
    above = (g, (z + 1) % ring)
    below = (g, (z + ring - 1) % ring)
    partner = (column * PAIR + (1 - half), z)

    def column_at(offset):
        return (column + offset) % columns

    def in_column(offset):
        return (column_at(offset) * PAIR + half, z)

    load_state = pltpu.make_async_copy(init_ref, state_0, load_sem.at[0])
    load_cond = pltpu.make_async_copy(cond_ref, cond, load_sem.at[1])
    load_cond.start()
    load_state.start()

    barrier = pltpu.get_barrier_semaphore()
    others = [above, below, partner] + [in_column(o) for o in range(1, columns)]
    for other in others:
        pl.semaphore_signal(barrier, inc=1, device_id=other, device_id_type=MESH)
    pl.semaphore_wait(barrier, len(others))

    def remote(src, dst, send, recv, where):
        return pltpu.make_async_remote_copy(
            src_ref=src, dst_ref=dst, send_sem=send, recv_sem=recv,
            device_id=where, device_id_type=MESH)

    def rim_up(level, chunk):
        who = pl.ds(chunk * CHUNK, CHUNK)
        src = init_ref.at[who, last] if level == 0 else state[level].at[who, last]
        return remote(src, lo_in.at[level, who], rim_send.at[level, chunk, 0],
                      rim_recv.at[level, chunk, 0], above)

    def rim_down(level, chunk):
        who = pl.ds(chunk * CHUNK, CHUNK)
        src = init_ref.at[who, 0] if level == 0 else state[level].at[who, 0]
        return remote(src, hi_in.at[level, who], rim_send.at[level, chunk, 1],
                      rim_recv.at[level, chunk, 1], below)

    cond_up = remote(cond_ref.at[:, last], cond_lo, cond_sem.at[0], cond_sem.at[2], above)
    cond_down = remote(cond_ref.at[:, 0], cond_hi, cond_sem.at[1], cond_sem.at[3], below)
    cond_up.start()
    cond_down.start()

    @pl.loop(0, chunks)
    def _(chunk):
        rim_up(0, chunk).start()
        rim_down(0, chunk).start()

    load_cond.wait()
    row = lax.broadcasted_iota(jnp.int32, (nx, ny), 0)
    lane = lax.broadcasted_iota(jnp.int32, (nx, ny), 1)
    x_open = jnp.where(row < nx - 1, HALF_STEP, 0.0)
    y_open = jnp.where(lane < ny - 1, HALF_STEP, 0.0)
    lo_open = jnp.where(z > 0, HALF_STEP, 0.0).astype(jnp.float32)
    hi_open = jnp.where(z < ring - 1, HALF_STEP, 0.0).astype(jnp.float32)
    ends = (jnp.where(row == 0, HALF_STEP, 0.0) + jnp.where(row == nx - 1, HALF_STEP, 0.0)
            + jnp.where(lane == 0, HALF_STEP, 0.0) + jnp.where(lane == ny - 1, HALF_STEP, 0.0))

    @pl.loop(0, fields)
    def _(f):
        for layer in range(layers):
            k = cond[f, layer]
            x_hi = (k + pltpu.roll(k, nx - 1, 0)) * x_open
            y_hi = (k + pltpu.roll(k, ny - 1, 1)) * y_open
            x_lo = pltpu.roll(x_hi, 1, 0)
            y_lo = pltpu.roll(y_hi, 1, 1)
            cx[f, layer, 0] = x_hi
            cx[f, layer, 1] = x_lo
            cy[f, layer, 0] = y_hi
            cy[f, layer, 1] = y_lo
            keep[f, layer] = (1.0 - k * ends) - ((x_hi + x_lo) + (y_hi + y_lo))
            if layer < last:
                cz[f, layer + 1] = (k + cond[f, layer + 1]) * HALF_STEP

    load_state.wait()
    cond_up.wait_recv()
    cond_down.wait_recv()

    @pl.loop(0, fields)
    def _(f):
        cz[f, 0] = (cond[f, 0] + cond_lo[f]) * lo_open
        cz[f, layers] = (cond[f, last] + cond_hi[f]) * hi_open
        keep[f, 0] = keep[f, 0] - cond[f, 0] * (HALF_STEP - lo_open)
        keep[f, last] = keep[f, last] - cond[f, last] * (HALF_STEP - hi_open)
        for layer in range(layers):
            keep[f, layer] = keep[f, layer] - (cz[f, layer] + cz[f, layer + 1])

    def advanced(level, member, layer):
        f = seeds_ref[0, member]
        now = state[level]
        u = now[member, layer]
        down = lo_in[level, member] if layer == 0 else now[member, layer - 1]
        up = hi_in[level, member] if layer == last else now[member, layer + 1]
        along_z = cz[f, layer + 1] * up + cz[f, layer] * down
        along_x = cx[f, layer, 0] * pltpu.roll(u, nx - 1, 0) + cx[f, layer, 1] * pltpu.roll(u, 1, 0)
        along_y = cy[f, layer, 0] * pltpu.roll(u, ny - 1, 1) + cy[f, layer, 1] * pltpu.roll(u, 1, 1)
        return (keep[f, layer] * u + along_z) + (along_x + along_y)

    def advance(level, member, which):
        for layer, cells in [(layer, advanced(level, member, layer)) for layer in which]:
            state[level + 1][member, layer] = cells

    for level in range(STEPS - 1):
        @pl.loop(0, chunks)
        def _(chunk, level=level):
            rim_up(level, chunk).wait_recv()
            rim_down(level, chunk).wait_recv()
            for i in range(CHUNK):
                member = chunk * CHUNK + i
                advance(level, member, range(layers))
            rim_up(level + 1, chunk).start()
            if level + 1 < STEPS - 1:
                rim_down(level + 1, chunk).start()

    @pl.loop(0, chunks)
    def _(chunk):
        rim_down(STEPS - 1, chunk).start()

    def count_of(group):
        return counts_ref[group].astype(jnp.float32)

    tile = (share, ny)
    own = count_of(g)

    def collect(layer):
        inverse = jnp.full(tile, 1.0, jnp.float32) / own

        @pl.loop(0, columns)
        def _(c):
            for h in range(PAIR):
                rows = pl.ds((c * PAIR + h) * share, share)
                total = jnp.zeros(tile, jnp.float32)
                for m in range(members):
                    live = jnp.where(m < counts_ref[g], 1.0, 0.0).astype(jnp.float32)
                    total = total + live * state_4[m, layer, rows]
                mean = total * inverse
                s2 = jnp.zeros(tile, jnp.float32)
                s3 = jnp.zeros(tile, jnp.float32)
                s4 = jnp.zeros(tile, jnp.float32)
                for m in range(members):
                    live = jnp.where(m < counts_ref[g], 1.0, 0.0).astype(jnp.float32)
                    d = (state_4[m, layer, rows] - mean) * live
                    dd = d * d
                    s2 = s2 + dd
                    s3 = s3 + dd * d
                    s4 = s4 + dd * dd
                sums[layer, c, h, 0] = mean
                sums[layer, c, h, 1] = s2
                sums[layer, c, h, 2] = s3
                sums[layer, c, h, 3] = s4

        for o in range(1, columns):
            over_x(layer, o).start()

    def over_x(layer, o):
        return remote(sums.at[layer, column_at(o)], got_x.at[layer, o - 1],
                      x_send.at[layer, o - 1], x_recv.at[layer, o - 1], in_column(o))

    def over_y(layer):
        return remote(part.at[layer, 1 - half], got_y.at[layer], y_send.at[layer], y_recv.at[layer], partner)

    def chan(left, right):
        na, ma, a2, a3, a4 = left
        nb, mb, b2, b3, b4 = right
        total = na + nb
        delta = mb - ma
        ratio = delta / total
        mean = ma + ratio * nb
        cross = delta * ratio * (na * nb)
        m2 = a2 + b2 + cross
        m3 = a3 + b3 + cross * ratio * (na - nb) + 3.0 * ratio * (na * b2 - nb * a2)
        m4 = (a4 + b4 + cross * ratio * ratio * (na * na - na * nb + nb * nb)
              + 6.0 * ratio * ratio * (na * na * b2 + nb * nb * a2)
              + 4.0 * ratio * (na * b3 - nb * a3))
        return total, mean, m2, m3, m4

    def column_count(h):
        total = count_of(h)
        for c in range(1, columns):
            total = total + count_of(c * PAIR + h)
        return total

    def merge_x(layer):
        for o in range(1, columns):
            over_x(layer, o).wait_recv()
        for h in range(PAIR):
            merged = (own, *[sums[layer, column, h, s] for s in range(4)])
            for o in range(1, columns):
                n = count_of(column_at(columns - o) * PAIR + half)
                merged = chan(merged, (n, *[got_x[layer, o - 1, h, s] for s in range(4)]))
            for s in range(4):
                part[layer, h, s] = merged[1 + s]
        over_y(layer).start()

    def merge_y(layer):
        over_y(layer).wait_recv()
        left = (column_count(half), *[part[layer, half, s] for s in range(4)])
        right = (column_count(1 - half), *[got_y[layer, s] for s in range(4)])
        total, mean, m2, m3, m4 = chan(left, right)
        inverse = jnp.full(tile, 1.0, jnp.float32) / total
        out_ref[0, layer] = mean
        out_ref[1, layer] = m2 * inverse
        out_ref[2, layer] = m3 * inverse
        out_ref[3, layer] = m4 * inverse

    inner = list(range(1, last))

    @pl.loop(0, members)
    def _(member):
        advance(STEPS - 1, member, inner)

    for layer in inner:
        collect(layer)

    @pl.loop(0, chunks)
    def _(chunk):
        rim_up(STEPS - 1, chunk).wait_recv()
        for i in range(CHUNK):
            member = chunk * CHUNK + i
            advance(STEPS - 1, member, [0])

    collect(0)
    for layer in inner:
        merge_x(layer)

    @pl.loop(0, chunks)
    def _(chunk):
        rim_down(STEPS - 1, chunk).wait_recv()
        for i in range(CHUNK):
            member = chunk * CHUNK + i
            advance(STEPS - 1, member, [last])

    collect(last)
    merge_x(0)
    for layer in inner:
        merge_y(layer)
    merge_x(last)
    merge_y(0)
    merge_y(last)

    cond_up.wait_send()
    cond_down.wait_send()
    for level in range(STEPS):
        @pl.loop(0, chunks)
        def _(chunk, level=level):
            rim_up(level, chunk).wait_send()
            rim_down(level, chunk).wait_send()
    for layer in range(layers):
        for o in range(1, columns):
            over_x(layer, o).wait_send()
        over_y(layer).wait_send()


def shards(groups, ring, init_fields, conductivity, seeds, counts):
    _, members, layers, nx, ny = init_fields.shape
    fields = conductivity.shape[0]
    columns = groups // PAIR
    share = nx // groups
    chunks = members // CHUNK
    f32 = jnp.float32
    out = jax.ShapeDtypeStruct((4, layers, share, ny), f32)
    vmem = pltpu.VMEM
    dma = pltpu.SemaphoreType.DMA
    moments = pl.pallas_call(
        functools.partial(kernel, groups, ring),
        out_shape=out,
        in_specs=[
            pl.BlockSpec(memory_space=pltpu.SMEM),
            pl.BlockSpec(memory_space=pltpu.SMEM),
            pl.BlockSpec(memory_space=pl.ANY),
            pl.BlockSpec(memory_space=pl.ANY),
        ],
        out_specs=pl.BlockSpec(memory_space=pltpu.VMEM),
        scratch_shapes=[
            *[vmem((members, layers, nx, ny), f32)] * (STEPS + 1),
            vmem((STEPS, members, nx, ny), f32),
            vmem((STEPS, members, nx, ny), f32),
            vmem((fields, layers, nx, ny), f32),
            vmem((fields, nx, ny), f32),
            vmem((fields, nx, ny), f32),
            vmem((fields, layers + 1, nx, ny), f32),
            vmem((fields, layers, 2, nx, ny), f32),
            vmem((fields, layers, 2, nx, ny), f32),
            vmem((fields, layers, nx, ny), f32),
            vmem((layers, columns, PAIR, 4, share, ny), f32),
            vmem((layers, columns - 1, PAIR, 4, share, ny), f32),
            vmem((layers, PAIR, 4, share, ny), f32),
            vmem((layers, 4, share, ny), f32),
            dma((2,)),
            dma((4,)),
            dma((STEPS, chunks, 2)),
            dma((STEPS, chunks, 2)),
            dma((layers, columns - 1)),
            dma((layers, columns - 1)),
            dma((layers,)),
            dma((layers,)),
        ],
        compiler_params=pltpu.CompilerParams(
            collective_id=0, has_side_effects=True, vmem_limit_bytes=60 * 1024 * 1024),
    )(seeds, counts, init_fields[0], conductivity)
    return tuple(moments[i] for i in range(4))


def solution(mesh):
    return jax.shard_map(
        functools.partial(shards, mesh.shape["grp"], mesh.shape["gz"]),
        mesh=mesh,
        in_specs=(P("grp", None, "gz", None, None), P(None, "gz", None, None), P("grp", None), P()),
        out_specs=(P("gz", "grp", None),) * 4,
        check_vma=False,
    )
```

```python
import functools

import jax
import jax.numpy as jnp
from jax import lax
from jax.experimental import pallas as pl
from jax.experimental.pallas import tpu as pltpu
from jax.sharding import PartitionSpec as P

STEPS = 4
PAIR = 2
CHUNK = 4
HALF_STEP = 0.15 * 0.5
MESH = pl.DeviceIdType.MESH


def kernel(groups, ring, seeds_ref, counts_ref, init_ref, cond_ref,
           out_ref,
           state_0, state_1, state_2, state_3, state_4, lo_in, hi_in,
           cond, cond_lo, cond_hi, cz, cx, cy, keep,
           sums, got_x, part, got_y,
           load_sem, cond_sem, rim_send, rim_recv, x_send, x_recv, y_send, y_recv):
    members, layers, nx, ny = init_ref.shape
    fields = cond_ref.shape[0]
    columns = groups // PAIR
    share = nx // groups
    chunks = members // CHUNK
    last = layers - 1
    state = (state_0, state_1, state_2, state_3, state_4)
    g = lax.axis_index("grp")
    z = lax.axis_index("gz")
    column, half = g // PAIR, g % PAIR
    above = (g, (z + 1) % ring)
    below = (g, (z + ring - 1) % ring)
    partner = (column * PAIR + (1 - half), z)

    def column_at(offset):
        return (column + offset) % columns

    def in_column(offset):
        return (column_at(offset) * PAIR + half, z)

    load_state = pltpu.make_async_copy(init_ref, state_0, load_sem.at[0])
    load_cond = pltpu.make_async_copy(cond_ref, cond, load_sem.at[1])
    load_cond.start()
    load_state.start()

    barrier = pltpu.get_barrier_semaphore()
    others = [above, below, partner] + [in_column(o) for o in range(1, columns)]
    for other in others:
        pl.semaphore_signal(barrier, inc=1, device_id=other, device_id_type=MESH)
    pl.semaphore_wait(barrier, len(others))

    def remote(src, dst, send, recv, where):
        return pltpu.make_async_remote_copy(
            src_ref=src, dst_ref=dst, send_sem=send, recv_sem=recv,
            device_id=where, device_id_type=MESH)

    def rim_up(level, chunk):
        who = pl.ds(chunk * CHUNK, CHUNK)
        src = init_ref.at[who, last] if level == 0 else state[level].at[who, last]
        return remote(src, lo_in.at[level, who], rim_send.at[level, chunk, 0],
                      rim_recv.at[level, chunk, 0], above)

    def rim_down(level, chunk):
        who = pl.ds(chunk * CHUNK, CHUNK)
        src = init_ref.at[who, 0] if level == 0 else state[level].at[who, 0]
        return remote(src, hi_in.at[level, who], rim_send.at[level, chunk, 1],
                      rim_recv.at[level, chunk, 1], below)

    cond_up = remote(cond_ref.at[:, last], cond_lo, cond_sem.at[0], cond_sem.at[2], above)
    cond_down = remote(cond_ref.at[:, 0], cond_hi, cond_sem.at[1], cond_sem.at[3], below)
    cond_up.start()
    cond_down.start()

    @pl.loop(0, chunks)
    def _(chunk):
        rim_up(0, chunk).start()
        rim_down(0, chunk).start()

    load_cond.wait()
    row = lax.broadcasted_iota(jnp.int32, (nx, ny), 0)
    lane = lax.broadcasted_iota(jnp.int32, (nx, ny), 1)
    x_open = jnp.where(row < nx - 1, HALF_STEP, 0.0)
    y_open = jnp.where(lane < ny - 1, HALF_STEP, 0.0)
    lo_open = jnp.where(z > 0, HALF_STEP, 0.0).astype(jnp.float32)
    hi_open = jnp.where(z < ring - 1, HALF_STEP, 0.0).astype(jnp.float32)
    ends = (jnp.where(row == 0, HALF_STEP, 0.0) + jnp.where(row == nx - 1, HALF_STEP, 0.0)
            + jnp.where(lane == 0, HALF_STEP, 0.0) + jnp.where(lane == ny - 1, HALF_STEP, 0.0))

    @pl.loop(0, fields)
    def _(f):
        for layer in range(layers):
            k = cond[f, layer]
            x_hi = (k + pltpu.roll(k, nx - 1, 0)) * x_open
            y_hi = (k + pltpu.roll(k, ny - 1, 1)) * y_open
            x_lo = pltpu.roll(x_hi, 1, 0)
            y_lo = pltpu.roll(y_hi, 1, 1)
            cx[f, layer, 0] = x_hi
            cx[f, layer, 1] = x_lo
            cy[f, layer, 0] = y_hi
            cy[f, layer, 1] = y_lo
            keep[f, layer] = (1.0 - k * ends) - ((x_hi + x_lo) + (y_hi + y_lo))
            if layer < last:
                cz[f, layer + 1] = (k + cond[f, layer + 1]) * HALF_STEP

    load_state.wait()
    cond_up.wait_recv()
    cond_down.wait_recv()

    @pl.loop(0, fields)
    def _(f):
        cz[f, 0] = (cond[f, 0] + cond_lo[f]) * lo_open
        cz[f, layers] = (cond[f, last] + cond_hi[f]) * hi_open
        keep[f, 0] = keep[f, 0] - cond[f, 0] * (HALF_STEP - lo_open)
        keep[f, last] = keep[f, last] - cond[f, last] * (HALF_STEP - hi_open)
        for layer in range(layers):
            keep[f, layer] = keep[f, layer] - (cz[f, layer] + cz[f, layer + 1])

    def advanced(level, member, layer):
        f = seeds_ref[0, member]
        now = state[level]
        u = now[member, layer]
        down = lo_in[level, member] if layer == 0 else now[member, layer - 1]
        up = hi_in[level, member] if layer == last else now[member, layer + 1]
        along_z = cz[f, layer + 1] * up + cz[f, layer] * down
        along_x = cx[f, layer, 0] * pltpu.roll(u, nx - 1, 0) + cx[f, layer, 1] * pltpu.roll(u, 1, 0)
        along_y = cy[f, layer, 0] * pltpu.roll(u, ny - 1, 1) + cy[f, layer, 1] * pltpu.roll(u, 1, 1)
        return (keep[f, layer] * u + along_z) + (along_x + along_y)

    def advance(level, member, which):
        for layer, cells in [(layer, advanced(level, member, layer)) for layer in which]:
            state[level + 1][member, layer] = cells

    for level in range(STEPS - 1):
        @pl.loop(0, chunks)
        def _(chunk, level=level):
            rim_up(level, chunk).wait_recv()
            rim_down(level, chunk).wait_recv()
            for i in range(CHUNK):
                member = chunk * CHUNK + i
                advance(level, member, range(layers))
            rim_up(level + 1, chunk).start()
            if level + 1 < STEPS - 1:
                rim_down(level + 1, chunk).start()

    @pl.loop(0, chunks)
    def _(chunk):
        rim_down(STEPS - 1, chunk).start()

    def count_of(group):
        return counts_ref[group].astype(jnp.float32)

    tile = (share, ny)
    own = count_of(g)

    def collect(layer):
        inverse = jnp.full(tile, 1.0, jnp.float32) / own

        @pl.loop(0, columns)
        def _(c):
            for h in range(PAIR):
                rows = pl.ds((c * PAIR + h) * share, share)
                total = jnp.zeros(tile, jnp.float32)
                for m in range(members):
                    live = jnp.where(m < counts_ref[g], 1.0, 0.0).astype(jnp.float32)
                    total = total + live * state_4[m, layer, rows]
                mean = total * inverse
                s2 = jnp.zeros(tile, jnp.float32)
                s3 = jnp.zeros(tile, jnp.float32)
                s4 = jnp.zeros(tile, jnp.float32)
                for m in range(members):
                    live = jnp.where(m < counts_ref[g], 1.0, 0.0).astype(jnp.float32)
                    d = (state_4[m, layer, rows] - mean) * live
                    dd = d * d
                    s2 = s2 + dd
                    s3 = s3 + dd * d
                    s4 = s4 + dd * dd
                sums[layer, c, h, 0] = mean
                sums[layer, c, h, 1] = s2
                sums[layer, c, h, 2] = s3
                sums[layer, c, h, 3] = s4

        for o in range(1, columns):
            over_x(layer, o).start()

    def over_x(layer, o):
        return remote(sums.at[layer, column_at(o)], got_x.at[layer, o - 1],
                      x_send.at[layer, o - 1], x_recv.at[layer, o - 1], in_column(o))

    def over_y(layer):
        return remote(part.at[layer, 1 - half], got_y.at[layer], y_send.at[layer], y_recv.at[layer], partner)

    def chan(left, right):
        na, ma, a2, a3, a4 = left
        nb, mb, b2, b3, b4 = right
        total = na + nb
        delta = mb - ma
        ratio = delta / total
        mean = ma + ratio * nb
        cross = delta * ratio * (na * nb)
        m2 = a2 + b2 + cross
        m3 = a3 + b3 + cross * ratio * (na - nb) + 3.0 * ratio * (na * b2 - nb * a2)
        m4 = (a4 + b4 + cross * ratio * ratio * (na * na - na * nb + nb * nb)
              + 6.0 * ratio * ratio * (na * na * b2 + nb * nb * a2)
              + 4.0 * ratio * (na * b3 - nb * a3))
        return total, mean, m2, m3, m4

    def column_count(h):
        total = count_of(h)
        for c in range(1, columns):
            total = total + count_of(c * PAIR + h)
        return total

    def merge_x(layer):
        for o in range(1, columns):
            over_x(layer, o).wait_recv()
        for h in range(PAIR):
            merged = (own, *[sums[layer, column, h, s] for s in range(4)])
            for o in range(1, columns):
                n = count_of(column_at(columns - o) * PAIR + half)
                merged = chan(merged, (n, *[got_x[layer, o - 1, h, s] for s in range(4)]))
            for s in range(4):
                part[layer, h, s] = merged[1 + s]
        over_y(layer).start()

    def merge_y(layer):
        over_y(layer).wait_recv()
        left = (column_count(half), *[part[layer, half, s] for s in range(4)])
        right = (column_count(1 - half), *[got_y[layer, s] for s in range(4)])
        total, mean, m2, m3, m4 = chan(left, right)
        inverse = jnp.full(tile, 1.0, jnp.float32) / total
        out_ref[0, layer] = mean
        out_ref[1, layer] = m2 * inverse
        out_ref[2, layer] = m3 * inverse
        out_ref[3, layer] = m4 * inverse

    inner = list(range(1, last))

    @pl.loop(0, members)
    def _(member):
        advance(STEPS - 1, member, inner)

    for layer in inner:
        collect(layer)

    @pl.loop(0, chunks)
    def _(chunk):
        rim_up(STEPS - 1, chunk).wait_recv()
        for i in range(CHUNK):
            member = chunk * CHUNK + i
            advance(STEPS - 1, member, [0])

    collect(0)
    for layer in inner:
        merge_x(layer)

    @pl.loop(0, chunks)
    def _(chunk):
        rim_down(STEPS - 1, chunk).wait_recv()
        for i in range(CHUNK):
            member = chunk * CHUNK + i
            advance(STEPS - 1, member, [last])

    collect(last)
    merge_x(0)
    for layer in inner:
        merge_y(layer)
    merge_x(last)
    merge_y(0)
    merge_y(last)

    cond_up.wait_send()
    cond_down.wait_send()
    for level in range(STEPS):
        @pl.loop(0, chunks)
        def _(chunk, level=level):
            rim_up(level, chunk).wait_send()
            rim_down(level, chunk).wait_send()
    for layer in range(layers):
        for o in range(1, columns):
            over_x(layer, o).wait_send()
        over_y(layer).wait_send()


def shards(groups, ring, init_fields, conductivity, seeds, counts):
    _, members, layers, nx, ny = init_fields.shape
    fields = conductivity.shape[0]
    columns = groups // PAIR
    share = nx // groups
    chunks = members // CHUNK
    f32 = jnp.float32
    out = jax.ShapeDtypeStruct((4, layers, share, ny), f32)
    vmem = pltpu.VMEM
    dma = pltpu.SemaphoreType.DMA
    moments = pl.pallas_call(
        functools.partial(kernel, groups, ring),
        out_shape=out,
        in_specs=[
            pl.BlockSpec(memory_space=pltpu.SMEM),
            pl.BlockSpec(memory_space=pltpu.SMEM),
            pl.BlockSpec(memory_space=pl.ANY),
            pl.BlockSpec(memory_space=pl.ANY),
        ],
        out_specs=pl.BlockSpec(memory_space=pltpu.VMEM),
        scratch_shapes=[
            *[vmem((members, layers, nx, ny), f32)] * (STEPS + 1),
            vmem((STEPS, members, nx, ny), f32),
            vmem((STEPS, members, nx, ny), f32),
            vmem((fields, layers, nx, ny), f32),
            vmem((fields, nx, ny), f32),
            vmem((fields, nx, ny), f32),
            vmem((fields, layers + 1, nx, ny), f32),
            vmem((fields, layers, 2, nx, ny), f32),
            vmem((fields, layers, 2, nx, ny), f32),
            vmem((fields, layers, nx, ny), f32),
            vmem((layers, columns, PAIR, 4, share, ny), f32),
            vmem((layers, columns - 1, PAIR, 4, share, ny), f32),
            vmem((layers, PAIR, 4, share, ny), f32),
            vmem((layers, 4, share, ny), f32),
            dma((2,)),
            dma((4,)),
            dma((STEPS, chunks, 2)),
            dma((STEPS, chunks, 2)),
            dma((layers, columns - 1)),
            dma((layers, columns - 1)),
            dma((layers,)),
            dma((layers,)),
        ],
        compiler_params=pltpu.CompilerParams(
            collective_id=0, has_side_effects=True, vmem_limit_bytes=60 * 1024 * 1024),
    )(seeds, counts, init_fields[0], conductivity)
    return tuple(moments[i] for i in range(4))


def solution(mesh):
    return jax.shard_map(
        functools.partial(shards, mesh.shape["grp"], mesh.shape["gz"]),
        mesh=mesh,
        in_specs=(P("grp", None, "gz", None, None), P(None, "gz", None, None), P("grp", None), P()),
        out_specs=(P("gz", "grp", None),) * 4,
        check_vma=False,
    )
```

```python
import functools

import jax
import jax.numpy as jnp
from jax import lax
from jax.experimental import pallas as pl
from jax.experimental.pallas import tpu as pltpu
from jax.sharding import PartitionSpec as P

STEPS = 4
PAIR = 2
RUN = 8
CHUNK = 3
HALF_STEP = 0.15 * 0.5
MESH = pl.DeviceIdType.MESH


def kernel(groups, ring, seeds_ref, counts_ref, init_ref, cond_ref,
           out_ref,
           state_0, state_1, state_2, state_3, state_4, lo_in, hi_in,
           cond, cond_lo, cond_hi, cz, cx, cy, keep,
           sums, got_x, part, got_y,
           load_sem, cond_sem, rim_send, rim_recv, x_send, x_recv, y_send, y_recv):
    members, layers, nx, ny = init_ref.shape
    fields = cond_ref.shape[0]
    columns = groups // PAIR
    share = nx // groups
    chunks = members // CHUNK
    last = layers - 1
    state = (state_0, state_1, state_2, state_3, state_4)
    g = lax.axis_index("grp")
    z = lax.axis_index("gz")
    column, half = g // PAIR, g % PAIR
    inner = list(range(1, last))
    z_above, z_below = (z + 1) % ring, (z + ring - 1) % ring
    partner_group = column * PAIR + (1 - half)
    above, below, partner = (g, z_above), (g, z_below), (partner_group, z)
    even = z % 2 == 0
    odd = jnp.logical_not(even)
    cond_above = (jnp.where(z % RUN == RUN - 1, partner_group, g), z_above)
    cond_below = (jnp.where(z % RUN == 0, partner_group, g), z_below)

    def column_at(offset):
        return (column + offset) % columns

    def in_column(offset):
        return (column_at(offset) * PAIR + half, z)

    load_state = pltpu.make_async_copy(init_ref, state_0, load_sem.at[0])
    load_cond = pltpu.make_async_copy(cond_ref, cond, load_sem.at[1])
    load_cond.start()
    load_state.start()

    barrier = pltpu.get_barrier_semaphore()
    others = [above, below, partner, (partner_group, z_above), (partner_group, z_below)]
    others += [in_column(o) for o in range(1, columns)]
    for other in others:
        pl.semaphore_signal(barrier, inc=1, device_id=other, device_id_type=MESH)
    pl.semaphore_wait(barrier, len(others))

    def remote(src, dst, send, recv, where):
        return pltpu.make_async_remote_copy(
            src_ref=src, dst_ref=dst, send_sem=send, recv_sem=recv,
            device_id=where, device_id_type=MESH)

    def rim_up(level, chunk):
        who = pl.ds(chunk * CHUNK, CHUNK)
        src = init_ref.at[who, last] if level == 0 else state[level].at[who, last]
        return remote(src, lo_in.at[level, who], rim_send.at[level, chunk, 0],
                      rim_recv.at[level, chunk, 0], above)

    def rim_down(level, chunk):
        who = pl.ds(chunk * CHUNK, CHUNK)
        src = init_ref.at[who, 0] if level == 0 else state[level].at[who, 0]
        return remote(src, hi_in.at[level, who], rim_send.at[level, chunk, 1],
                      rim_recv.at[level, chunk, 1], below)

    cond_up = remote(cond_ref.at[:, last], cond_lo, cond_sem.at[0], cond_sem.at[2], cond_above)
    cond_down = remote(cond_ref.at[:, 0], cond_hi, cond_sem.at[1], cond_sem.at[3], cond_below)
    cond_up.start()
    cond_down.start()

    @pl.loop(0, chunks)
    def _(chunk):
        rim_up(0, chunk).start()
        rim_down(0, chunk).start()

    load_cond.wait()
    row = lax.broadcasted_iota(jnp.int32, (nx, ny), 0)
    lane = lax.broadcasted_iota(jnp.int32, (nx, ny), 1)
    x_open = jnp.where(row < nx - 1, HALF_STEP, 0.0)
    y_open = jnp.where(lane < ny - 1, HALF_STEP, 0.0)
    lo_open = jnp.where(z > 0, HALF_STEP, 0.0).astype(jnp.float32)
    hi_open = jnp.where(z < ring - 1, HALF_STEP, 0.0).astype(jnp.float32)
    ends = (jnp.where(row == 0, HALF_STEP, 0.0) + jnp.where(row == nx - 1, HALF_STEP, 0.0)
            + jnp.where(lane == 0, HALF_STEP, 0.0) + jnp.where(lane == ny - 1, HALF_STEP, 0.0))

    @pl.loop(0, fields)
    def _(f):
        for layer in range(layers):
            k = cond[f, layer]
            x_hi = (k + pltpu.roll(k, nx - 1, 0)) * x_open
            y_hi = (k + pltpu.roll(k, ny - 1, 1)) * y_open
            x_lo = pltpu.roll(x_hi, 1, 0)
            y_lo = pltpu.roll(y_hi, 1, 1)
            cx[f, layer, 0] = x_hi
            cx[f, layer, 1] = x_lo
            cy[f, layer, 0] = y_hi
            cy[f, layer, 1] = y_lo
            keep[f, layer] = (1.0 - k * ends) - ((x_hi + x_lo) + (y_hi + y_lo))
            if layer < last:
                cz[f, layer + 1] = (k + cond[f, layer + 1]) * HALF_STEP

    load_state.wait()
    cond_up.wait_recv()
    cond_down.wait_recv()

    @pl.loop(0, fields)
    def _(f):
        cz[f, 0] = (cond[f, 0] + cond_lo[f]) * lo_open
        cz[f, layers] = (cond[f, last] + cond_hi[f]) * hi_open
        keep[f, 0] = keep[f, 0] - cond[f, 0] * (HALF_STEP - lo_open)
        keep[f, last] = keep[f, last] - cond[f, last] * (HALF_STEP - hi_open)
        for layer in range(layers):
            keep[f, layer] = keep[f, layer] - (cz[f, layer] + cz[f, layer + 1])

    def advanced(level, member, layer):
        f = seeds_ref[0, member]
        now = state[level]
        u = now[member, layer]
        down = lo_in[level, member] if layer == 0 else now[member, layer - 1]
        up = hi_in[level, member] if layer == last else now[member, layer + 1]
        along_z = cz[f, layer + 1] * up + cz[f, layer] * down
        along_x = cx[f, layer, 0] * pltpu.roll(u, nx - 1, 0) + cx[f, layer, 1] * pltpu.roll(u, 1, 0)
        along_y = cy[f, layer, 0] * pltpu.roll(u, ny - 1, 1) + cy[f, layer, 1] * pltpu.roll(u, 1, 1)
        return (keep[f, layer] * u + along_z) + (along_x + along_y)

    def advance(level, member, which):
        for layer, cells in [(layer, advanced(level, member, layer)) for layer in which]:
            state[level + 1][member, layer] = cells

    def members_in(chunk):
        return [chunk * CHUNK + i for i in range(CHUNK)]

    def lower(level, chunk):
        rim_up(level, chunk).wait_recv()
        for member in members_in(chunk):
            advance(level, member, [0, 1] if level == 1 else [0])
        if level + 1 < STEPS:
            rim_down(level + 1, chunk).start()

    def upper(level, chunk):
        rim_down(level, chunk).wait_recv()
        for member in members_in(chunk):
            advance(level, member, [last, last - 1] if level == 1 else [last])
        if level + 1 < STEPS:
            rim_up(level + 1, chunk).start()

    def near(level, chunk):
        pl.when(even)(lambda: upper(level, chunk))
        pl.when(odd)(lambda: lower(level, chunk))

    def far(level, chunk):
        pl.when(even)(lambda: lower(level, chunk))
        pl.when(odd)(lambda: upper(level, chunk))

    @pl.loop(0, chunks)
    def _(chunk):
        for member in members_in(chunk):
            advance(0, member, inner)
        near(0, chunk)

    for level in range(STEPS - 1):
        @pl.loop(0, chunks)
        def _(chunk, level=level):
            far(level, chunk)
            if level + 1 < STEPS - 1:
                near(level + 1, chunk)

    def count_of(group):
        return counts_ref[group].astype(jnp.float32)

    tile = (share, ny)
    own = count_of(g)

    def collect(layer):
        inverse = jnp.full(tile, 1.0, jnp.float32) / own

        @pl.loop(0, columns)
        def _(c):
            for h in range(PAIR):
                rows = pl.ds((c * PAIR + h) * share, share)
                total = jnp.zeros(tile, jnp.float32)
                for m in range(members):
                    live = jnp.where(m < counts_ref[g], 1.0, 0.0).astype(jnp.float32)
                    total = total + live * state_4[m, layer, rows]
                mean = total * inverse
                s2 = jnp.zeros(tile, jnp.float32)
                s3 = jnp.zeros(tile, jnp.float32)
                s4 = jnp.zeros(tile, jnp.float32)
                for m in range(members):
                    live = jnp.where(m < counts_ref[g], 1.0, 0.0).astype(jnp.float32)
                    d = (state_4[m, layer, rows] - mean) * live
                    dd = d * d
                    s2 = s2 + dd
                    s3 = s3 + dd * d
                    s4 = s4 + dd * dd
                sums[layer, c, h, 0] = mean
                sums[layer, c, h, 1] = s2
                sums[layer, c, h, 2] = s3
                sums[layer, c, h, 3] = s4

        for o in range(1, columns):
            over_x(layer, o).start()

    def over_x(layer, o):
        return remote(sums.at[layer, column_at(o)], got_x.at[layer, o - 1],
                      x_send.at[layer, o - 1], x_recv.at[layer, o - 1], in_column(o))

    def over_y(layer):
        return remote(part.at[layer, 1 - half], got_y.at[layer], y_send.at[layer], y_recv.at[layer], partner)

    def chan(left, right):
        na, ma, a2, a3, a4 = left
        nb, mb, b2, b3, b4 = right
        total = na + nb
        delta = mb - ma
        ratio = delta / total
        mean = ma + ratio * nb
        cross = delta * ratio * (na * nb)
        m2 = a2 + b2 + cross
        m3 = a3 + b3 + cross * ratio * (na - nb) + 3.0 * ratio * (na * b2 - nb * a2)
        m4 = (a4 + b4 + cross * ratio * ratio * (na * na - na * nb + nb * nb)
              + 6.0 * ratio * ratio * (na * na * b2 + nb * nb * a2)
              + 4.0 * ratio * (na * b3 - nb * a3))
        return total, mean, m2, m3, m4

    def column_count(h):
        total = count_of(h)
        for c in range(1, columns):
            total = total + count_of(c * PAIR + h)
        return total

    def merge_x(layer):
        for o in range(1, columns):
            over_x(layer, o).wait_recv()
        for h in range(PAIR):
            merged = (own, *[sums[layer, column, h, s] for s in range(4)])
            for o in range(1, columns):
                n = count_of(column_at(columns - o) * PAIR + half)
                merged = chan(merged, (n, *[got_x[layer, o - 1, h, s] for s in range(4)]))
            for s in range(4):
                part[layer, h, s] = merged[1 + s]
        over_y(layer).start()

    def merge_y(layer):
        over_y(layer).wait_recv()
        left = (column_count(half), *[part[layer, half, s] for s in range(4)])
        right = (column_count(1 - half), *[got_y[layer, s] for s in range(4)])
        total, mean, m2, m3, m4 = chan(left, right)
        inverse = jnp.full(tile, 1.0, jnp.float32) / total
        out_ref[0, layer] = mean
        out_ref[1, layer] = m2 * inverse
        out_ref[2, layer] = m3 * inverse
        out_ref[3, layer] = m4 * inverse

    @pl.loop(0, chunks)
    def _(chunk):
        for member in members_in(chunk):
            advance(STEPS - 2, member, inner)
        for member in members_in(chunk):
            advance(STEPS - 1, member, inner)

    for layer in inner:
        collect(layer)

    @pl.loop(0, chunks)
    def _(chunk):
        near(STEPS - 1, chunk)

    near_layer, far_layer = jnp.where(even, last, 0), jnp.where(even, 0, last)
    collect(near_layer)
    for layer in inner:
        merge_x(layer)

    @pl.loop(0, chunks)
    def _(chunk):
        far(STEPS - 1, chunk)

    collect(far_layer)
    merge_x(near_layer)
    for layer in inner:
        merge_y(layer)
    merge_x(far_layer)
    merge_y(near_layer)
    merge_y(far_layer)

    cond_up.wait_send()
    cond_down.wait_send()
    for level in range(STEPS):
        @pl.loop(0, chunks)
        def _(chunk, level=level):
            rim_up(level, chunk).wait_send()
            rim_down(level, chunk).wait_send()
    for layer in range(layers):
        for o in range(1, columns):
            over_x(layer, o).wait_send()
        over_y(layer).wait_send()


def shards(groups, ring, init_fields, conductivity, seeds, counts):
    _, members, layers, nx, ny = init_fields.shape
    fields = conductivity.shape[0]
    columns = groups // PAIR
    share = nx // groups
    chunks = members // CHUNK
    f32 = jnp.float32
    out = jax.ShapeDtypeStruct((4, layers, share, ny), f32)
    vmem = pltpu.VMEM
    dma = pltpu.SemaphoreType.DMA
    moments = pl.pallas_call(
        functools.partial(kernel, groups, ring),
        out_shape=out,
        in_specs=[
            pl.BlockSpec(memory_space=pltpu.SMEM),
            pl.BlockSpec(memory_space=pltpu.SMEM),
            pl.BlockSpec(memory_space=pl.ANY),
            pl.BlockSpec(memory_space=pl.ANY),
        ],
        out_specs=pl.BlockSpec(memory_space=pltpu.VMEM),
        scratch_shapes=[
            *[vmem((members, layers, nx, ny), f32)] * (STEPS + 1),
            vmem((STEPS, members, nx, ny), f32),
            vmem((STEPS, members, nx, ny), f32),
            vmem((fields, layers, nx, ny), f32),
            vmem((fields, nx, ny), f32),
            vmem((fields, nx, ny), f32),
            vmem((fields, layers + 1, nx, ny), f32),
            vmem((fields, layers, 2, nx, ny), f32),
            vmem((fields, layers, 2, nx, ny), f32),
            vmem((fields, layers, nx, ny), f32),
            vmem((layers, columns, PAIR, 4, share, ny), f32),
            vmem((layers, columns - 1, PAIR, 4, share, ny), f32),
            vmem((layers, PAIR, 4, share, ny), f32),
            vmem((layers, 4, share, ny), f32),
            dma((2,)),
            dma((4,)),
            dma((STEPS, chunks, 2)),
            dma((STEPS, chunks, 2)),
            dma((layers, columns - 1)),
            dma((layers, columns - 1)),
            dma((layers,)),
            dma((layers,)),
        ],
        compiler_params=pltpu.CompilerParams(
            collective_id=0, has_side_effects=True, vmem_limit_bytes=60 * 1024 * 1024),
    )(seeds, counts, init_fields[0], conductivity)
    return tuple(moments[i] for i in range(4))


def solution(mesh):
    return jax.shard_map(
        functools.partial(shards, mesh.shape["grp"], mesh.shape["gz"]),
        mesh=mesh,
        in_specs=(P("grp", None, "gz", None, None), P(None, "gz", None, None), P("grp", None), P()),
        out_specs=(P("gz", "grp", None),) * 4,
        check_vma=False,
    )
```

```python
import functools

import jax
import jax.numpy as jnp
from jax import lax
from jax.experimental import pallas as pl
from jax.experimental.pallas import tpu as pltpu
from jax.sharding import PartitionSpec as P

STEPS = 4
PAIR = 2
RUN = 8
CHUNK = 3
HALF_STEP = 0.15 * 0.5
MESH = pl.DeviceIdType.MESH


def kernel(groups, ring, seeds_ref, counts_ref, init_ref, cond_ref,
           out_ref,
           state_0, state_1, state_2, state_3, state_4, lo_in, hi_in,
           cond, cond_lo, cond_hi, cz, cx, cy, keep,
           sums, got_x, part, got_y, got_all,
           load_sem, cond_sem, rim_send, rim_recv, x_send, x_recv, y_send, y_recv, all_send, all_recv):
    members, layers, nx, ny = init_ref.shape
    fields = cond_ref.shape[0]
    columns = groups // PAIR
    share = nx // groups
    chunks = members // CHUNK
    last = layers - 1
    state = (state_0, state_1, state_2, state_3, state_4)
    g = lax.axis_index("grp")
    z = lax.axis_index("gz")
    column, half = g // PAIR, g % PAIR
    inner = list(range(1, last))
    z_above, z_below = (z + 1) % ring, (z + ring - 1) % ring
    partner_group = column * PAIR + (1 - half)
    above, below, partner = (g, z_above), (g, z_below), (partner_group, z)
    even = z % 2 == 0
    odd = jnp.logical_not(even)
    has_above, has_below = z < ring - 1, z > 0
    jump_above = jnp.logical_and(z % RUN == RUN - 1, has_above)
    jump_below = jnp.logical_and(z % RUN == 0, has_below)
    cond_above = (jnp.where(jump_above, partner_group, g), z_above)
    cond_below = (jnp.where(jump_below, partner_group, g), z_below)

    def column_at(offset):
        return (column + offset) % columns

    def in_column(offset):
        return (column_at(offset) * PAIR + half, z)

    offsets = [(o, flip) for o in range(columns) for flip in range(PAIR) if o or flip]

    def group_at(offset, flip):
        return (column_at(offset) * PAIR + (1 - half if flip else half), z)

    load_state = pltpu.make_async_copy(init_ref, state_0, load_sem.at[0])
    load_cond = pltpu.make_async_copy(cond_ref, cond, load_sem.at[1])
    load_cond.start()
    load_state.start()

    barrier = pltpu.get_barrier_semaphore()
    others = [group_at(o, flip) for o, flip in offsets]

    def greet(other):
        pl.semaphore_signal(barrier, inc=1, device_id=other, device_id_type=MESH)

    for other in others:
        greet(other)
    pl.when(has_above)(lambda: greet(above))
    pl.when(has_below)(lambda: greet(below))
    pl.when(jump_above)(lambda: greet(cond_above))
    pl.when(jump_below)(lambda: greet(cond_below))
    expected = len(others)
    for also in (has_above, has_below, jump_above, jump_below):
        expected = expected + jnp.where(also, 1, 0)
    pl.semaphore_wait(barrier, expected)

    def remote(src, dst, send, recv, where):
        return pltpu.make_async_remote_copy(
            src_ref=src, dst_ref=dst, send_sem=send, recv_sem=recv,
            device_id=where, device_id_type=MESH)

    def rim_up(level, chunk):
        who = pl.ds(chunk * CHUNK, CHUNK)
        src = init_ref.at[who, last] if level == 0 else state[level].at[who, last]
        return remote(src, lo_in.at[level, who], rim_send.at[level, chunk, 0],
                      rim_recv.at[level, chunk, 0], above)

    def rim_down(level, chunk):
        who = pl.ds(chunk * CHUNK, CHUNK)
        src = init_ref.at[who, 0] if level == 0 else state[level].at[who, 0]
        return remote(src, hi_in.at[level, who], rim_send.at[level, chunk, 1],
                      rim_recv.at[level, chunk, 1], below)

    cond_up = remote(cond_ref.at[:, last], cond_lo, cond_sem.at[0], cond_sem.at[2], cond_above)
    cond_down = remote(cond_ref.at[:, 0], cond_hi, cond_sem.at[1], cond_sem.at[3], cond_below)

    start, sent, arrived = (lambda c: c.start()), (lambda c: c.wait_send()), (lambda c: c.wait_recv())

    def up(act, copy):
        pl.when(has_below if act is arrived else has_above)(lambda: act(copy))

    def down(act, copy):
        pl.when(has_above if act is arrived else has_below)(lambda: act(copy))

    up(start, cond_up)
    down(start, cond_down)

    def first_rims(which):
        @pl.loop(0, chunks)
        def _(chunk):
            if which == "up":
                up(start, rim_up(0, chunk))
            else:
                down(start, rim_down(0, chunk))

    pl.when(jump_above)(lambda: first_rims("up"))
    pl.when(jump_below)(lambda: first_rims("down"))
    pl.when(even)(lambda: first_rims("up"))
    pl.when(odd)(lambda: first_rims("down"))

    def no_halo(side, cond_side):
        cond_side[...] = jnp.zeros_like(cond_side)

        @pl.loop(0, members)
        def _(member):
            for level in range(STEPS):
                side[level, member] = jnp.zeros((nx, ny), jnp.float32)

    pl.when(jnp.logical_not(has_below))(lambda: no_halo(lo_in, cond_lo))
    pl.when(jnp.logical_not(has_above))(lambda: no_halo(hi_in, cond_hi))

    load_cond.wait()
    row = lax.broadcasted_iota(jnp.int32, (nx, ny), 0)
    lane = lax.broadcasted_iota(jnp.int32, (nx, ny), 1)
    x_open = jnp.where(row < nx - 1, HALF_STEP, 0.0)
    y_open = jnp.where(lane < ny - 1, HALF_STEP, 0.0)
    lo_open = jnp.where(z > 0, HALF_STEP, 0.0).astype(jnp.float32)
    hi_open = jnp.where(z < ring - 1, HALF_STEP, 0.0).astype(jnp.float32)
    ends = (jnp.where(row == 0, HALF_STEP, 0.0) + jnp.where(row == nx - 1, HALF_STEP, 0.0)
            + jnp.where(lane == 0, HALF_STEP, 0.0) + jnp.where(lane == ny - 1, HALF_STEP, 0.0))

    @pl.loop(0, fields)
    def _(f):
        for layer in range(layers):
            k = cond[f, layer]
            x_hi = (k + pltpu.roll(k, nx - 1, 0)) * x_open
            y_hi = (k + pltpu.roll(k, ny - 1, 1)) * y_open
            x_lo = pltpu.roll(x_hi, 1, 0)
            y_lo = pltpu.roll(y_hi, 1, 1)
            cx[f, layer, 0] = x_hi
            cx[f, layer, 1] = x_lo
            cy[f, layer, 0] = y_hi
            cy[f, layer, 1] = y_lo
            keep[f, layer] = (1.0 - k * ends) - ((x_hi + x_lo) + (y_hi + y_lo))
            if layer < last:
                cz[f, layer + 1] = (k + cond[f, layer + 1]) * HALF_STEP

    pl.when(jnp.logical_and(odd, jnp.logical_not(jump_above)))(lambda: first_rims("up"))
    pl.when(jnp.logical_and(even, jnp.logical_not(jump_below)))(lambda: first_rims("down"))

    load_state.wait()
    up(arrived, cond_up)
    down(arrived, cond_down)

    @pl.loop(0, fields)
    def _(f):
        cz[f, 0] = (cond[f, 0] + cond_lo[f]) * lo_open
        cz[f, layers] = (cond[f, last] + cond_hi[f]) * hi_open
        keep[f, 0] = keep[f, 0] - cond[f, 0] * (HALF_STEP - lo_open)
        keep[f, last] = keep[f, last] - cond[f, last] * (HALF_STEP - hi_open)
        for layer in range(layers):
            keep[f, layer] = keep[f, layer] - (cz[f, layer] + cz[f, layer + 1])

    def advanced(level, member, layer):
        f = seeds_ref[0, member]
        now = state[level]
        u = now[member, layer]
        down = lo_in[level, member] if layer == 0 else now[member, layer - 1]
        up = hi_in[level, member] if layer == last else now[member, layer + 1]
        along_z = cz[f, layer + 1] * up + cz[f, layer] * down
        along_x = cx[f, layer, 0] * pltpu.roll(u, nx - 1, 0) + cx[f, layer, 1] * pltpu.roll(u, 1, 0)
        along_y = cy[f, layer, 0] * pltpu.roll(u, ny - 1, 1) + cy[f, layer, 1] * pltpu.roll(u, 1, 1)
        return (keep[f, layer] * u + along_z) + (along_x + along_y)

    def advance(level, member, which):
        for layer, cells in [(layer, advanced(level, member, layer)) for layer in which]:
            state[level + 1][member, layer] = cells

    def members_in(chunk):
        return [chunk * CHUNK + i for i in range(CHUNK)]

    def lower(level, chunk):
        up(arrived, rim_up(level, chunk))
        for member in members_in(chunk):
            advance(level, member, [0, 1] if level == 1 else [0])
        if level + 1 < STEPS:
            down(start, rim_down(level + 1, chunk))

    def upper(level, chunk):
        down(arrived, rim_down(level, chunk))
        for member in members_in(chunk):
            advance(level, member, [last, last - 1] if level == 1 else [last])
        if level + 1 < STEPS:
            up(start, rim_up(level + 1, chunk))

    def near(level, chunk):
        pl.when(even)(lambda: upper(level, chunk))
        pl.when(odd)(lambda: lower(level, chunk))

    def far(level, chunk):
        pl.when(even)(lambda: lower(level, chunk))
        pl.when(odd)(lambda: upper(level, chunk))

    @pl.loop(0, chunks)
    def _(chunk):
        for member in members_in(chunk):
            advance(0, member, inner)
        near(0, chunk)

    for level in range(STEPS - 1):
        @pl.loop(0, chunks)
        def _(chunk, level=level):
            far(level, chunk)
            if level + 1 < STEPS - 1:
                near(level + 1, chunk)

    def count_of(group):
        return counts_ref[group].astype(jnp.float32)

    tile = (share, ny)
    own = count_of(g)

    def collect(layer):
        inverse = jnp.full(tile, 1.0, jnp.float32) / own

        @pl.loop(0, columns)
        def _(c):
            for h in range(PAIR):
                rows = pl.ds((c * PAIR + h) * share, share)
                total = jnp.zeros(tile, jnp.float32)
                for m in range(members):
                    live = jnp.where(m < counts_ref[g], 1.0, 0.0).astype(jnp.float32)
                    total = total + live * state_4[m, layer, rows]
                mean = total * inverse
                s2 = jnp.zeros(tile, jnp.float32)
                s3 = jnp.zeros(tile, jnp.float32)
                s4 = jnp.zeros(tile, jnp.float32)
                for m in range(members):
                    live = jnp.where(m < counts_ref[g], 1.0, 0.0).astype(jnp.float32)
                    d = (state_4[m, layer, rows] - mean) * live
                    dd = d * d
                    s2 = s2 + dd
                    s3 = s3 + dd * d
                    s4 = s4 + dd * dd
                sums[layer, c, h, 0] = mean
                sums[layer, c, h, 1] = s2
                sums[layer, c, h, 2] = s3
                sums[layer, c, h, 3] = s4

    def send_over_x(layer):
        for o in range(1, columns):
            over_x(layer, o).start()

    def over_x(layer, o):
        return remote(sums.at[layer, column_at(o)], got_x.at[layer, o - 1],
                      x_send.at[layer, o - 1], x_recv.at[layer, o - 1], in_column(o))

    def to_group(layer, at):
        o, flip = offsets[at]
        return remote(sums.at[layer, column_at(o), 1 - half if flip else half], got_all.at[at],
                      all_send.at[at], all_recv.at[at], group_at(o, flip))

    def over_y(layer):
        return remote(part.at[layer, 1 - half], got_y.at[layer], y_send.at[layer], y_recv.at[layer], partner)

    def chan(left, right):
        na, ma, a2, a3, a4 = left
        nb, mb, b2, b3, b4 = right
        total = na + nb
        delta = mb - ma
        ratio = delta / total
        mean = ma + ratio * nb
        cross = delta * ratio * (na * nb)
        m2 = a2 + b2 + cross
        m3 = a3 + b3 + cross * ratio * (na - nb) + 3.0 * ratio * (na * b2 - nb * a2)
        m4 = (a4 + b4 + cross * ratio * ratio * (na * na - na * nb + nb * nb)
              + 6.0 * ratio * ratio * (na * na * b2 + nb * nb * a2)
              + 4.0 * ratio * (na * b3 - nb * a3))
        return total, mean, m2, m3, m4

    def column_count(h):
        total = count_of(h)
        for c in range(1, columns):
            total = total + count_of(c * PAIR + h)
        return total

    def merge_x(layer):
        for o in range(1, columns):
            over_x(layer, o).wait_recv()
        for h in range(PAIR):
            merged = (own, *[sums[layer, column, h, s] for s in range(4)])
            for o in range(1, columns):
                n = count_of(column_at(columns - o) * PAIR + half)
                merged = chan(merged, (n, *[got_x[layer, o - 1, h, s] for s in range(4)]))
            for s in range(4):
                part[layer, h, s] = merged[1 + s]
        over_y(layer).start()

    def merge_y(layer):
        over_y(layer).wait_recv()
        left = (column_count(half), *[part[layer, half, s] for s in range(4)])
        right = (column_count(1 - half), *[got_y[layer, s] for s in range(4)])
        finish(layer, chan(left, right))

    def merge_all(layer):
        parts = [(own, *[sums[layer, column, half, s] for s in range(4)])]
        for at, (o, flip) in enumerate(offsets):
            to_group(layer, at).wait_recv()
            n = count_of(column_at(columns - o) * PAIR + (1 - half if flip else half))
            parts.append((n, *[got_all[at, s] for s in range(4)]))
        while len(parts) > 1:
            parts = [chan(a, b) for a, b in zip(parts[::2], parts[1::2])]
        finish(layer, parts[0])

    def finish(layer, merged):
        total, mean, m2, m3, m4 = merged
        inverse = jnp.full(tile, 1.0, jnp.float32) / total
        out_ref[0, layer] = mean
        out_ref[1, layer] = m2 * inverse
        out_ref[2, layer] = m3 * inverse
        out_ref[3, layer] = m4 * inverse

    @pl.loop(0, chunks)
    def _(chunk):
        for member in members_in(chunk):
            advance(STEPS - 2, member, inner)
        for member in members_in(chunk):
            advance(STEPS - 1, member, inner)

    for layer in inner:
        collect(layer)
        send_over_x(layer)

    @pl.loop(0, chunks)
    def _(chunk):
        near(STEPS - 1, chunk)

    near_layer, far_layer = jnp.where(even, last, 0), jnp.where(even, 0, last)
    collect(near_layer)
    send_over_x(near_layer)
    for layer in inner:
        merge_x(layer)

    @pl.loop(0, chunks)
    def _(chunk):
        far(STEPS - 1, chunk)

    collect(far_layer)
    for at in range(len(offsets)):
        to_group(far_layer, at).start()
    merge_x(near_layer)
    for layer in inner:
        merge_y(layer)
    merge_y(near_layer)
    merge_all(far_layer)

    up(sent, cond_up)
    down(sent, cond_down)
    for level in range(STEPS):
        @pl.loop(0, chunks)
        def _(chunk, level=level):
            up(sent, rim_up(level, chunk))
            down(sent, rim_down(level, chunk))
    for layer in inner + [near_layer]:
        for o in range(1, columns):
            over_x(layer, o).wait_send()
        over_y(layer).wait_send()
    for at in range(len(offsets)):
        to_group(far_layer, at).wait_send()


def shards(groups, ring, init_fields, conductivity, seeds, counts):
    _, members, layers, nx, ny = init_fields.shape
    fields = conductivity.shape[0]
    columns = groups // PAIR
    share = nx // groups
    chunks = members // CHUNK
    f32 = jnp.float32
    out = jax.ShapeDtypeStruct((4, layers, share, ny), f32)
    vmem = pltpu.VMEM
    dma = pltpu.SemaphoreType.DMA
    moments = pl.pallas_call(
        functools.partial(kernel, groups, ring),
        out_shape=out,
        in_specs=[
            pl.BlockSpec(memory_space=pltpu.SMEM),
            pl.BlockSpec(memory_space=pltpu.SMEM),
            pl.BlockSpec(memory_space=pl.ANY),
            pl.BlockSpec(memory_space=pl.ANY),
        ],
        out_specs=pl.BlockSpec(memory_space=pltpu.VMEM),
        scratch_shapes=[
            *[vmem((members, layers, nx, ny), f32)] * (STEPS + 1),
            vmem((STEPS, members, nx, ny), f32),
            vmem((STEPS, members, nx, ny), f32),
            vmem((fields, layers, nx, ny), f32),
            vmem((fields, nx, ny), f32),
            vmem((fields, nx, ny), f32),
            vmem((fields, layers + 1, nx, ny), f32),
            vmem((fields, layers, 2, nx, ny), f32),
            vmem((fields, layers, 2, nx, ny), f32),
            vmem((fields, layers, nx, ny), f32),
            vmem((layers, columns, PAIR, 4, share, ny), f32),
            vmem((layers, columns - 1, PAIR, 4, share, ny), f32),
            vmem((layers, PAIR, 4, share, ny), f32),
            vmem((layers, 4, share, ny), f32),
            vmem((groups - 1, 4, share, ny), f32),
            dma((2,)),
            dma((4,)),
            dma((STEPS, chunks, 2)),
            dma((STEPS, chunks, 2)),
            dma((layers, columns - 1)),
            dma((layers, columns - 1)),
            dma((layers,)),
            dma((layers,)),
            dma((groups - 1,)),
            dma((groups - 1,)),
        ],
        compiler_params=pltpu.CompilerParams(
            collective_id=0, has_side_effects=True, vmem_limit_bytes=60 * 1024 * 1024),
    )(seeds, counts, init_fields[0], conductivity)
    return tuple(moments[i] for i in range(4))


def solution(mesh):
    return jax.shard_map(
        functools.partial(shards, mesh.shape["grp"], mesh.shape["gz"]),
        mesh=mesh,
        in_specs=(P("grp", None, "gz", None, None), P(None, "gz", None, None), P("grp", None), P()),
        out_specs=(P("gz", "grp", None),) * 4,
        check_vma=False,
    )
```

```python
import functools

import jax
import jax.numpy as jnp
from jax import lax
from jax.experimental import pallas as pl
from jax.experimental.pallas import tpu as pltpu
from jax.sharding import PartitionSpec as P

STEPS = 4
PAIR = 2
RUN = 8
CHUNK = 2
AHEAD = 2
DEEP = 3
HALF_STEP = 0.15 * 0.5
MESH = pl.DeviceIdType.MESH


def kernel(groups, ring, seeds_ref, counts_ref, init_ref, cond_ref,
           out_ref,
           state_0, state_1, state_2, state_3, state_4, side_in, deep, deep_1,
           cond, cond_in, cond_deep, cz, cx, cy, keep, deep_cz, deep_cx, deep_cy, deep_keep,
           sums, got_x, part, got_y,
           load_sem, cond_sem, rim_send, rim_recv, deep_send, deep_recv, x_send, x_recv, y_send, y_recv):
    members, layers, nx, ny = init_ref.shape
    fields = cond_ref.shape[0]
    columns = groups // PAIR
    share = nx // groups
    chunks = members // CHUNK
    last = layers - 1
    state = (state_0, state_1, state_2, state_3, state_4)
    g = lax.axis_index("grp")
    z = lax.axis_index("gz")
    column, half = g // PAIR, g % PAIR
    inner = list(range(1, last))
    z_above, z_below = (z + 1) % ring, (z + ring - 1) % ring
    partner_group = column * PAIR + (1 - half)
    above, below, partner = (g, z_above), (g, z_below), (partner_group, z)
    even = z % 2 == 0
    odd = jnp.logical_not(even)
    has_above, has_below = z < ring - 1, z > 0
    jump_above = jnp.logical_and(z % RUN == RUN - 1, has_above)
    jump_below = jnp.logical_and(z % RUN == 0, has_below)
    jump = jnp.logical_or(jump_above, jump_below)
    stay = jnp.logical_not(jump)
    far_side = jnp.where(jump_below, 0, 1)
    z_far = jnp.where(jump_below, z_below, z_above)

    def column_at(offset):
        return (column + offset) % columns

    def in_column(offset):
        return (column_at(offset) * PAIR + half, z)

    load_state = pltpu.make_async_copy(init_ref, state_0, load_sem.at[0])
    load_cond = pltpu.make_async_copy(cond_ref, cond, load_sem.at[1])
    load_cond.start()
    load_state.start()

    barrier = pltpu.get_barrier_semaphore()
    others = [partner] + [in_column(o) for o in range(1, columns)]

    def greet(other):
        pl.semaphore_signal(barrier, inc=1, device_id=other, device_id_type=MESH)

    for other in others:
        greet(other)
    pl.when(has_above)(lambda: greet(above))
    pl.when(has_below)(lambda: greet(below))
    pl.when(jump)(lambda: greet((partner_group, z_far)))
    expected = len(others)
    for also in (has_above, has_below, jump):
        expected = expected + jnp.where(also, 1, 0)
    pl.semaphore_wait(barrier, expected)

    def remote(src, dst, send, recv, where):
        return pltpu.make_async_remote_copy(
            src_ref=src, dst_ref=dst, send_sem=send, recv_sem=recv,
            device_id=where, device_id_type=MESH)

    def rim_up(level, chunk):
        who = pl.ds(chunk * CHUNK, CHUNK)
        src = init_ref.at[who, last] if level == 0 else state[level].at[who, last]
        return remote(src, side_in.at[0, level, who], rim_send.at[level, chunk, 0],
                      rim_recv.at[level, chunk, 0], above)

    def rim_down(level, chunk):
        who = pl.ds(chunk * CHUNK, CHUNK)
        src = init_ref.at[who, 0] if level == 0 else state[level].at[who, 0]
        return remote(src, side_in.at[1, level, who], rim_send.at[level, chunk, 1],
                      rim_recv.at[level, chunk, 1], below)

    cond_up = remote(cond_ref.at[:, last], cond_in.at[0], cond_sem.at[0], cond_sem.at[3], above)
    cond_down = remote(cond_ref.at[:, 0], cond_in.at[1], cond_sem.at[1], cond_sem.at[4], below)
    cond_swap = remote(cond_ref, cond_deep, cond_sem.at[2], cond_sem.at[5], (partner_group, z_far))

    def swap(chunk, first=0):
        who = pl.ds(chunk * CHUNK, CHUNK)
        return remote(init_ref.at[who, pl.ds(first, DEEP)], deep.at[who], deep_send.at[chunk],
                      deep_recv.at[chunk], (g, z_far))

    def start_swap(chunk):
        pl.when(jump_below)(lambda: swap(chunk).start())
        pl.when(jump_above)(lambda: swap(chunk, layers - DEEP).start())

    start, sent, arrived = (lambda c: c.start()), (lambda c: c.wait_send()), (lambda c: c.wait_recv())

    def rims_at(level):
        if level == STEPS - 1:
            return has_above, has_below
        return (jnp.logical_and(has_above, jnp.logical_not(jump_above)),
                jnp.logical_and(has_below, jnp.logical_not(jump_below)))

    def up(act, copy, level=0):
        above_too, below_too = rims_at(level)
        pl.when(below_too if act is arrived else above_too)(lambda: act(copy))

    def down(act, copy, level=0):
        above_too, below_too = rims_at(level)
        pl.when(above_too if act is arrived else below_too)(lambda: act(copy))

    @pl.when(jump)
    def _():
        for chunk in range(AHEAD):
            start_swap(chunk)
        cond_swap.start()

    up(start, cond_up)
    down(start, cond_down)

    def first_rims(way, rim):
        @pl.loop(0, chunks)
        def _(chunk):
            way(start, rim(0, chunk))

    pl.when(even)(lambda: first_rims(up, rim_up))
    pl.when(odd)(lambda: first_rims(down, rim_down))

    def no_halo(side):
        for f in range(fields):
            cond_in[side, f] = jnp.zeros((nx, ny), jnp.float32)

        @pl.loop(0, members)
        def _(member):
            for level in range(STEPS):
                side_in[side, level, member] = jnp.zeros((nx, ny), jnp.float32)

    pl.when(jnp.logical_not(has_below))(lambda: no_halo(0))
    pl.when(jnp.logical_not(has_above))(lambda: no_halo(1))

    load_cond.wait()
    row = lax.broadcasted_iota(jnp.int32, (nx, ny), 0)
    lane = lax.broadcasted_iota(jnp.int32, (nx, ny), 1)
    x_open = jnp.where(row < nx - 1, HALF_STEP, 0.0)
    y_open = jnp.where(lane < ny - 1, HALF_STEP, 0.0)
    lo_open = jnp.where(z > 0, HALF_STEP, 0.0).astype(jnp.float32)
    hi_open = jnp.where(z < ring - 1, HALF_STEP, 0.0).astype(jnp.float32)
    ends = (jnp.where(row == 0, HALF_STEP, 0.0) + jnp.where(row == nx - 1, HALF_STEP, 0.0)
            + jnp.where(lane == 0, HALF_STEP, 0.0) + jnp.where(lane == ny - 1, HALF_STEP, 0.0))

    def faces(k, along_x, along_y, f, layer):
        x_hi = (k + pltpu.roll(k, nx - 1, 0)) * x_open
        y_hi = (k + pltpu.roll(k, ny - 1, 1)) * y_open
        x_lo = pltpu.roll(x_hi, 1, 0)
        y_lo = pltpu.roll(y_hi, 1, 1)
        along_x[f, layer, 0] = x_hi
        along_x[f, layer, 1] = x_lo
        along_y[f, layer, 0] = y_hi
        along_y[f, layer, 1] = y_lo
        return (1.0 - k * ends) - ((x_hi + x_lo) + (y_hi + y_lo))

    @pl.loop(0, fields)
    def _(f):
        for layer in range(layers):
            k = cond[f, layer]
            keep[f, layer] = faces(k, cx, cy, f, layer)
            if layer < last:
                cz[f, layer + 1] = (k + cond[f, layer + 1]) * HALF_STEP

    pl.when(odd)(lambda: first_rims(up, rim_up))
    pl.when(even)(lambda: first_rims(down, rim_down))
    load_state.wait()

    def own(depth):
        return jnp.where(jump_below, depth, last - depth)

    def own_face(depth):
        return jnp.where(jump_below, depth, layers - depth)

    def far_cond(f, depth):
        return cond_deep[f, jnp.where(jump_below, last - depth, depth)]

    @pl.when(jump)
    def _():
        cond_swap.wait_recv()

        @pl.loop(0, fields)
        def _(f):
            before = cond[f, own(0)]
            for depth in range(DEEP - 1):
                k = far_cond(f, depth)
                rest = faces(k, deep_cx, deep_cy, f, depth)
                face_near = (before + k) * HALF_STEP
                face_far = (k + far_cond(f, depth + 1)) * HALF_STEP
                deep_cz[f, depth] = face_near
                deep_cz[f, depth + 1] = face_far
                deep_keep[f, depth] = rest - (face_near + face_far)
                before = k
            cond_in[far_side, f] = far_cond(f, 0)

    up(arrived, cond_up)
    down(arrived, cond_down)

    @pl.loop(0, fields)
    def _(f):
        cz[f, 0] = (cond[f, 0] + cond_in[0, f]) * lo_open
        cz[f, layers] = (cond[f, last] + cond_in[1, f]) * hi_open
        keep[f, 0] = keep[f, 0] - cond[f, 0] * (HALF_STEP - lo_open)
        keep[f, last] = keep[f, last] - cond[f, last] * (HALF_STEP - hi_open)
        for layer in range(layers):
            keep[f, layer] = keep[f, layer] - (cz[f, layer] + cz[f, layer + 1])

    def cell_step(u, kept, along_z, x_faces, y_faces):
        along_x = x_faces[0] * pltpu.roll(u, nx - 1, 0) + x_faces[1] * pltpu.roll(u, 1, 0)
        along_y = y_faces[0] * pltpu.roll(u, ny - 1, 1) + y_faces[1] * pltpu.roll(u, 1, 1)
        return (kept * u + along_z) + (along_x + along_y)

    def advanced(level, member, layer):
        f = seeds_ref[0, member]
        now = state[level]
        lower_cells = side_in[0, level, member] if layer == 0 else now[member, layer - 1]
        upper_cells = side_in[1, level, member] if layer == last else now[member, layer + 1]
        along_z = cz[f, layer + 1] * upper_cells + cz[f, layer] * lower_cells
        return cell_step(now[member, layer], keep[f, layer], along_z,
                         (cx[f, layer, 0], cx[f, layer, 1]), (cy[f, layer, 0], cy[f, layer, 1]))

    def own_advanced(level, member, depth):
        f = seeds_ref[0, member]
        now = state[level]
        at = own(depth)
        outer = side_in[far_side, level, member] if depth == 0 else now[member, own(depth - 1)]
        along_z = cz[f, own_face(depth)] * outer + cz[f, own_face(depth + 1)] * now[member, own(depth + 1)]
        return cell_step(now[member, at], keep[f, at], along_z,
                         (cx[f, at, 0], cx[f, at, 1]), (cy[f, at, 0], cy[f, at, 1]))

    def far_layer(level, member, depth):
        if level == 0:
            return deep[member, jnp.where(jump_below, DEEP - 1 - depth, depth)]
        return deep_1[member, depth]

    def far_advanced(level, member, depth):
        f = seeds_ref[0, member]
        inward = state[level][member, own(0)] if depth == 0 else far_layer(level, member, depth - 1)
        along_z = deep_cz[f, depth] * inward + deep_cz[f, depth + 1] * far_layer(level, member, depth + 1)
        return cell_step(far_layer(level, member, depth), deep_keep[f, depth], along_z,
                         (deep_cx[f, depth, 0], deep_cx[f, depth, 1]),
                         (deep_cy[f, depth, 0], deep_cy[f, depth, 1]))

    def far_chain(chunk):
        swap(chunk).wait_recv()
        pl.when(chunk + AHEAD < chunks)(lambda: start_swap(chunk + AHEAD))
        for i in range(CHUNK):
            member = chunk * CHUNK + i
            side_in[far_side, 0, member] = far_layer(0, member, 0)
            for level in range(DEEP):
                mine = [(d, own_advanced(level, member, d)) for d in range(2 if level == 1 else 1)]
                its = [(d, far_advanced(level, member, d)) for d in range(DEEP - 1 - level)]
                for depth, cells in mine:
                    state[level + 1][member, own(depth)] = cells
                for depth, cells in its:
                    if level == 0:
                        deep_1[member, depth] = cells
                    if depth == 0:
                        side_in[far_side, level + 1, member] = cells
        pl.when(jump_above)(lambda: rim_up(DEEP, chunk).start())
        pl.when(jump_below)(lambda: rim_down(DEEP, chunk).start())

    def advance(level, member, which):
        for layer, cells in [(layer, advanced(level, member, layer)) for layer in which]:
            state[level + 1][member, layer] = cells

    def members_in(chunk):
        return [chunk * CHUNK + i for i in range(CHUNK)]

    def lower(level, chunk):
        up(arrived, rim_up(level, chunk), level)
        for member in members_in(chunk):
            advance(level, member, [0, 1] if level == 1 else [0])
        if level + 1 < STEPS:
            down(start, rim_down(level + 1, chunk), level + 1)

    def upper(level, chunk):
        down(arrived, rim_down(level, chunk), level)
        for member in members_in(chunk):
            advance(level, member, [last, last - 1] if level == 1 else [last])
        if level + 1 < STEPS:
            up(start, rim_up(level + 1, chunk), level + 1)

    def near(level, chunk):
        pl.when(even)(lambda: upper(level, chunk))
        pl.when(odd)(lambda: lower(level, chunk))

    def far(level, chunk):
        pl.when(even)(lambda: lower(level, chunk))
        pl.when(odd)(lambda: upper(level, chunk))

    @pl.loop(0, chunks)
    def _(chunk):
        for member in members_in(chunk):
            advance(0, member, inner)
        near(0, chunk)

    for level in range(STEPS - 1):
        @pl.loop(0, chunks)
        def _(chunk, level=level):
            pl.when(stay)(lambda: far(level, chunk))
            if level == 1:
                pl.when(jump)(lambda: far_chain(chunk))
            if level + 1 < STEPS - 1:
                near(level + 1, chunk)

    def count_of(group):
        return counts_ref[group].astype(jnp.float32)

    tile = (share, ny)
    own = count_of(g)

    def collect(layer):
        inverse = jnp.full(tile, 1.0, jnp.float32) / own

        @pl.loop(0, columns)
        def _(c):
            for h in range(PAIR):
                rows = pl.ds((c * PAIR + h) * share, share)
                total = jnp.zeros(tile, jnp.float32)
                for m in range(members):
                    live = jnp.where(m < counts_ref[g], 1.0, 0.0).astype(jnp.float32)
                    total = total + live * state_4[m, layer, rows]
                mean = total * inverse
                s2 = jnp.zeros(tile, jnp.float32)
                s3 = jnp.zeros(tile, jnp.float32)
                s4 = jnp.zeros(tile, jnp.float32)
                for m in range(members):
                    live = jnp.where(m < counts_ref[g], 1.0, 0.0).astype(jnp.float32)
                    d = (state_4[m, layer, rows] - mean) * live
                    dd = d * d
                    s2 = s2 + dd
                    s3 = s3 + dd * d
                    s4 = s4 + dd * dd
                sums[layer, c, h, 0] = mean
                sums[layer, c, h, 1] = s2
                sums[layer, c, h, 2] = s3
                sums[layer, c, h, 3] = s4

        for o in range(1, columns):
            over_x(layer, o).start()

    def over_x(layer, o):
        return remote(sums.at[layer, column_at(o)], got_x.at[layer, o - 1],
                      x_send.at[layer, o - 1], x_recv.at[layer, o - 1], in_column(o))

    def over_y(layer):
        return remote(part.at[layer, 1 - half], got_y.at[layer], y_send.at[layer], y_recv.at[layer], partner)

    def chan(left, right):
        na, ma, a2, a3, a4 = left
        nb, mb, b2, b3, b4 = right
        total = na + nb
        delta = mb - ma
        ratio = delta / total
        mean = ma + ratio * nb
        cross = delta * ratio * (na * nb)
        m2 = a2 + b2 + cross
        m3 = a3 + b3 + cross * ratio * (na - nb) + 3.0 * ratio * (na * b2 - nb * a2)
        m4 = (a4 + b4 + cross * ratio * ratio * (na * na - na * nb + nb * nb)
              + 6.0 * ratio * ratio * (na * na * b2 + nb * nb * a2)
              + 4.0 * ratio * (na * b3 - nb * a3))
        return total, mean, m2, m3, m4

    def column_count(h):
        total = count_of(h)
        for c in range(1, columns):
            total = total + count_of(c * PAIR + h)
        return total

    def merge_x(layer):
        for o in range(1, columns):
            over_x(layer, o).wait_recv()
        for h in range(PAIR):
            merged = (own, *[sums[layer, column, h, s] for s in range(4)])
            for o in range(1, columns):
                n = count_of(column_at(columns - o) * PAIR + half)
                merged = chan(merged, (n, *[got_x[layer, o - 1, h, s] for s in range(4)]))
            for s in range(4):
                part[layer, h, s] = merged[1 + s]
        over_y(layer).start()

    def merge_y(layer):
        over_y(layer).wait_recv()
        left = (column_count(half), *[part[layer, half, s] for s in range(4)])
        right = (column_count(1 - half), *[got_y[layer, s] for s in range(4)])
        total, mean, m2, m3, m4 = chan(left, right)
        inverse = jnp.full(tile, 1.0, jnp.float32) / total
        out_ref[0, layer] = mean
        out_ref[1, layer] = m2 * inverse
        out_ref[2, layer] = m3 * inverse
        out_ref[3, layer] = m4 * inverse

    @pl.loop(0, chunks)
    def _(chunk):
        for member in members_in(chunk):
            advance(STEPS - 2, member, inner)
        for member in members_in(chunk):
            advance(STEPS - 1, member, inner)

    for layer in inner:
        collect(layer)

    @pl.loop(0, chunks)
    def _(chunk):
        near(STEPS - 1, chunk)

    near_layer, far_layer = jnp.where(even, last, 0), jnp.where(even, 0, last)
    collect(near_layer)
    for layer in inner:
        merge_x(layer)

    @pl.loop(0, chunks)
    def _(chunk):
        far(STEPS - 1, chunk)

    collect(far_layer)
    merge_x(near_layer)
    for layer in inner:
        merge_y(layer)
    merge_x(far_layer)
    merge_y(near_layer)
    merge_y(far_layer)

    @pl.when(jump)
    def _():
        cond_swap.wait_send()

        @pl.loop(0, chunks)
        def _(chunk):
            swap(chunk).wait_send()

    up(sent, cond_up)
    down(sent, cond_down)
    for level in range(STEPS):
        @pl.loop(0, chunks)
        def _(chunk, level=level):
            up(sent, rim_up(level, chunk), level)
            down(sent, rim_down(level, chunk), level)
    for layer in range(layers):
        for o in range(1, columns):
            over_x(layer, o).wait_send()
        over_y(layer).wait_send()


def shards(groups, ring, init_fields, conductivity, seeds, counts):
    _, members, layers, nx, ny = init_fields.shape
    fields = conductivity.shape[0]
    columns = groups // PAIR
    share = nx // groups
    chunks = members // CHUNK
    f32 = jnp.float32
    out = jax.ShapeDtypeStruct((4, layers, share, ny), f32)
    vmem = pltpu.VMEM
    dma = pltpu.SemaphoreType.DMA
    moments = pl.pallas_call(
        functools.partial(kernel, groups, ring),
        out_shape=out,
        in_specs=[
            pl.BlockSpec(memory_space=pltpu.SMEM),
            pl.BlockSpec(memory_space=pltpu.SMEM),
            pl.BlockSpec(memory_space=pl.ANY),
            pl.BlockSpec(memory_space=pl.ANY),
        ],
        out_specs=pl.BlockSpec(memory_space=pltpu.VMEM),
        scratch_shapes=[
            *[vmem((members, layers, nx, ny), f32)] * (STEPS + 1),
            vmem((2, STEPS, members, nx, ny), f32),
            vmem((members, DEEP, nx, ny), f32),
            vmem((members, DEEP - 1, nx, ny), f32),
            vmem((fields, layers, nx, ny), f32),
            vmem((2, fields, nx, ny), f32),
            vmem((fields, layers, nx, ny), f32),
            vmem((fields, layers + 1, nx, ny), f32),
            vmem((fields, layers, 2, nx, ny), f32),
            vmem((fields, layers, 2, nx, ny), f32),
            vmem((fields, layers, nx, ny), f32),
            vmem((fields, DEEP, nx, ny), f32),
            vmem((fields, DEEP - 1, 2, nx, ny), f32),
            vmem((fields, DEEP - 1, 2, nx, ny), f32),
            vmem((fields, DEEP - 1, nx, ny), f32),
            vmem((layers, columns, PAIR, 4, share, ny), f32),
            vmem((layers, columns - 1, PAIR, 4, share, ny), f32),
            vmem((layers, PAIR, 4, share, ny), f32),
            vmem((layers, 4, share, ny), f32),
            dma((2,)),
            dma((6,)),
            dma((STEPS, chunks, 2)),
            dma((STEPS, chunks, 2)),
            dma((chunks,)),
            dma((chunks,)),
            dma((layers, columns - 1)),
            dma((layers, columns - 1)),
            dma((layers,)),
            dma((layers,)),
        ],
        compiler_params=pltpu.CompilerParams(
            collective_id=0, has_side_effects=True, vmem_limit_bytes=60 * 1024 * 1024),
    )(seeds, counts, init_fields[0], conductivity)
    return tuple(moments[i] for i in range(4))


def solution(mesh):
    return jax.shard_map(
        functools.partial(shards, mesh.shape["grp"], mesh.shape["gz"]),
        mesh=mesh,
        in_specs=(P("grp", None, "gz", None, None), P(None, "gz", None, None), P("grp", None), P()),
        out_specs=(P("gz", "grp", None),) * 4,
        check_vma=False,
    )
```
